32 devices in a mesh: ens: 2 (over y), row: 4 (over z), col: 4 (over x, core).
Axes of the slice: x: 2, y: 2, z: 4, core: 2. Of those that a mesh axis runs over, the one named last changes fastest.
Arguments:
- series: float32 [24576, 256], P(('ens', 'row', 'col')), parts along dimension 0, may hold values from -22 to 22, as said below
- vectors: float32 [24576, 128], P(('ens', 'row', 'col')), parts along dimension 0, may hold values from -6 to 6
- damp_class: int32 [24576], P(('ens', 'row', 'col')), parts along dimension 0, may hold values from 0 to 15
- damp_levels: float32 [16], replicated, may hold values from 0.5 to 2
- removed_blocks: int32 [64, 32], P('ens'), parts along dimension 0, may hold values 0 or 1
Outputs:
- filtered: float32 [24576, 128], P(('ens', 'row', 'col')), parts along dimension 0
The draws below stay inside these ranges and needn't reach their ends.
There are 2 independent parts, one for each index of `ens`. The reference program is written for one: setup_inputs(seed, part) draws one part's arguments, and reference() takes and returns one part's arrays. A program takes and returns all parts, laid end to end along the dimension named above; an argument that names none is the same for every part. Nothing has to cross between parts.
Inputs may be any that keep to these rules, and one draw needn't show every extreme that they name: Each voxel's series is not constant.
All inputs are finite; a program needn't handle non-finite values.
Results may differ from the reference program's by a relative error of at most 0.0003.
Values sent between devices are 32-bit elements; how exact they have to be, the bound alone decides.
A program may use at most 128 MiB of HBM per device.

```python
import math
import jax
import jax.numpy as jnp
from jax import lax

N = 12288
S = 256
K = 128
G = 384
NCLASS = 16
NBLK = 32


def draw_series(key, part):
    drawn = jnp.clip(jax.random.normal(jax.random.fold_in(key, 11), (N, S), jnp.float32), -6.0, 6.0)
    return drawn


def touch_ends(result, own_key, low, top_value):
    longest = result.shape.index(max(result.shape))
    spots = []
    for shift in (0, 1):
        where = [jax.random.randint(jax.random.fold_in(own_key, axis), (), 0, length) for axis, length in enumerate(result.shape)]
        where[longest] = (where[longest] + shift) % result.shape[longest]
        spots.append(tuple(where))
    return result.at[spots[0]].set(low).at[spots[1]].set(top_value)


def levels(key, extent, split, smallest, high):
    gain, own = 1.0, jax.random.fold_in(key, 6)
    for dim, blocks in split:
        draws = jnp.exp(jax.random.uniform(jax.random.fold_in(own, dim), (blocks,), jnp.float32, smallest / len(split), high / len(split)))
        gain = gain * jnp.repeat(draws, extent[dim] // blocks).reshape([-1 if axis == dim else 1 for axis in range(len(extent))])
    return gain


def gaussian(rng, extent, width, reach, pieces=(), held_as=jnp.bfloat16):
    level = levels(rng, extent, pieces, -0.22, 0.18) if pieces else 1.0
    array = jax.random.normal(rng, extent, jnp.float32) * width * level
    return jnp.minimum(jnp.maximum(array, -reach), reach).astype(held_as)


def setup_inputs(seed: int = 0, part: int = 0) -> dict:
    key_of = jax.random.split(jax.random.key(seed), 6)
    part_splits = jax.random.split(jax.random.fold_in(key_of[5], part), 6)
    series = draw_series(jax.random.fold_in(jax.random.fold_in(key_of[5], part), 71), part)
    vectors = gaussian(part_splits[1], (N, K), 1.0, 6.0, ((0, 16),), jnp.float32)
    damp_class = touch_ends(jax.random.randint(part_splits[2], (N,), 0, NCLASS), jax.random.fold_in(part_splits[2], 1), 0, NCLASS - 1).astype(jnp.int32)
    damp_levels = jnp.clip(jnp.exp(jax.random.uniform(key_of[3], (NCLASS,), jnp.float32, math.log(0.5), math.log(2.0))), 0.5, 2.0)
    removed_blocks = touch_ends((jax.random.randint(part_splits[4], (NBLK, NBLK), 0, 8) < 1).astype(jnp.int32), jax.random.fold_in(part_splits[4], 1), 0, 1)
    return {"series": series, "vectors": vectors, "damp_class": damp_class, "damp_levels": damp_levels, "removed_blocks": removed_blocks}


sharpness = 12.0

def standardize(series):
    centered = series - lax.optimization_barrier(jnp.mean(series, axis=1, keepdims=True))
    spread = lax.optimization_barrier(jnp.mean(centered * centered, axis=1, keepdims=True))
    return centered * lax.rsqrt(spread + 1e-05)

def reference(series, vectors, damp_class, damp_levels, removed_blocks):
    z_all = standardize(series)
    onehot = (damp_class[:, None] == jnp.arange(NCLASS, dtype=jnp.int32)[None, :]).astype(jnp.float32)
    damping = lax.optimization_barrier(jnp.sum(onehot * damp_levels[None, :], axis=1))
    keep_all = 1.0 - removed_blocks.astype(jnp.float32)
    spectral_scale = 0.5 * N * jnp.mean(damp_levels * damp_levels)

    def normal_apply(field_in):

        def block_step(running, block_index):
            offset = (block_index * G).astype(jnp.int32)
            row_series = lax.dynamic_slice_in_dim(z_all, offset, G, 0)
            row_damp = lax.dynamic_slice_in_dim(damping, offset, G, 0)
            keep_row = jnp.repeat(lax.dynamic_slice_in_dim(keep_all, block_index.astype(jnp.int32), 1, 0), G, axis=1)
            correlation = jnp.dot(row_series, z_all.T, precision=lax.Precision.HIGHEST, preferred_element_type=jnp.float32) / S
            affinity = jnp.tanh(sharpness * correlation) * keep_row * row_damp[:, None]
            partial_value = jnp.dot(affinity, field_in, precision=lax.Precision.HIGHEST, preferred_element_type=jnp.float32)
            running = running + jnp.dot(affinity.T, partial_value, precision=lax.Precision.HIGHEST, preferred_element_type=jnp.float32)
            return (running, None)
        running, _ = lax.scan(block_step, jnp.zeros((N, K), jnp.float32), jnp.arange(N // G, dtype=jnp.int32))
        return running / spectral_scale
    first_term = normal_apply(vectors) - vectors
    return 2.0 * (normal_apply(first_term) - first_term) - vectors
```

```python
import jax
import jax.numpy as jnp
from jax import lax
from jax.sharding import PartitionSpec as P


sharpness = 12.0


def standardize(series):
    centered = series - jnp.mean(series, axis=1, keepdims=True)
    spread = jnp.mean(centered * centered, axis=1, keepdims=True)
    return centered * lax.rsqrt(spread + 1e-05)


def split(x):
    high = lax.reduce_precision(x, 8, 7)
    return high.astype(jnp.bfloat16), (x - high).astype(jnp.bfloat16)


def local(series, vectors, damp_class, damp_levels, removed_blocks):
    n_row, n_col = lax.axis_size("row"), lax.axis_size("col")
    row_id = lax.axis_index("row")
    col_id = lax.axis_index("col")
    shard_rows, samples = series.shape
    wide = vectors.shape[1]
    classes = damp_levels.shape[0]
    order = shard_rows * n_row * n_col
    z_own = standardize(series)
    onehot = (damp_class[:, None] == jnp.arange(classes, dtype=jnp.int32)[None, :]).astype(
        jnp.float32
    )
    damping = jnp.sum(onehot * damp_levels[None, :], axis=1)
    weight_own = damping * damping
    z_rows = lax.all_gather(z_own, "col", axis=0, tiled=True)
    z_cols = lax.all_gather(z_own, "row", axis=0, tiled=True)
    tile_rows, tile_cols = z_rows.shape[0], z_cols.shape[0]
    blocks = removed_blocks.shape[0]
    block_size = order // blocks
    row_block = (row_id * tile_rows + jnp.arange(tile_rows, dtype=jnp.int32)) // block_size
    position = jnp.arange(tile_cols, dtype=jnp.int32)
    col_index = (position // shard_rows * n_col + col_id) * shard_rows + position % shard_rows
    col_block = col_index // block_size
    keep = (1 - removed_blocks).astype(jnp.bfloat16)
    row_hot = (row_block[:, None] == jnp.arange(blocks)[None, :]).astype(jnp.bfloat16)
    col_hot = (col_block[:, None] == jnp.arange(blocks)[None, :]).astype(jnp.bfloat16)
    keep_rows = jnp.dot(row_hot, keep, preferred_element_type=jnp.float32).astype(jnp.bfloat16)
    rows_high, rows_low = split(z_rows)
    cols_high, cols_low = split(z_cols * (sharpness / samples))
    scores = lax.dot_general(
        jnp.concatenate([rows_high, rows_low, rows_high], axis=1),
        jnp.concatenate([cols_high, cols_high, cols_low], axis=1),
        (((1,), (1,)), ((), ())),
        preferred_element_type=jnp.float32,
    )
    keep_full = lax.dot_general(
        keep_rows, col_hot, (((1,), (1,)), ((), ())), preferred_element_type=jnp.float32
    )
    t_high, t_low = split(jnp.tanh(scores) * keep_full)
    spectral_scale = 0.5 * order * jnp.mean(damp_levels * damp_levels)

    def multiply(dims, field, fine):
        high, low = split(field)
        dims = ((dims, (0,)), ((), ()))
        both = lax.dot_general(
            t_high,
            jnp.concatenate([high, low], axis=1),
            dims,
            preferred_element_type=jnp.float32,
        )
        out = both[:, :wide] + both[:, wide:]
        if fine:
            out = out + lax.dot_general(t_low, high, dims, preferred_element_type=jnp.float32)
        return out

    def normal_apply(field_in, fine):
        product = multiply((1,), lax.all_gather(field_in, "row", axis=0, tiled=True), fine[0])
        product = lax.psum_scatter(product, "col", scatter_dimension=0, tiled=True)
        product = product * weight_own[:, None]
        returned = multiply((0,), lax.all_gather(product, "col", axis=0, tiled=True), fine[1])
        return lax.psum_scatter(returned, "row", scatter_dimension=0, tiled=True) / spectral_scale

    first_term = normal_apply(vectors, (True, False)) - vectors
    return 2.0 * (normal_apply(first_term, (False, True)) - first_term) - vectors


def solution(mesh):
    placed = (
        P(("ens", "row", "col"), None),
        P(("ens", "row", "col"), None),
        P(("ens", "row", "col")),
        P(),
        P("ens", None),
    )
    return jax.shard_map(
        local, mesh=mesh, in_specs=placed, out_specs=P(("ens", "row", "col"), None), check_vma=False
    )
```

```python
import functools

import jax
import jax.numpy as jnp
from jax import lax
from jax.experimental import pallas as pl
from jax.experimental.pallas import tpu as pltpu
from jax.sharding import PartitionSpec as P


sharpness = 12.0


def standardize(series):
    centered = series - jnp.mean(series, axis=1, keepdims=True)
    spread = jnp.mean(centered * centered, axis=1, keepdims=True)
    return centered * lax.rsqrt(spread + 1e-05)


def split(x):
    high = lax.reduce_precision(x, 8, 7)
    return high.astype(jnp.bfloat16), (x - high).astype(jnp.bfloat16)


MESH = pl.DeviceIdType.MESH


def send(src, dst, send_sem, recv_sem, device):
    return pltpu.make_async_remote_copy(
        src_ref=src,
        dst_ref=dst,
        send_sem=send_sem,
        recv_sem=recv_sem,
        device_id=device,
        device_id_type=MESH,
    )


def greet_line(n, me):
    barrier = pltpu.get_barrier_semaphore()

    @pl.when(me > 0)
    def _():
        pl.semaphore_signal(barrier, inc=1, device_id={"row": me - 1}, device_id_type=MESH)

    @pl.when(me < n - 1)
    def _():
        pl.semaphore_signal(barrier, inc=1, device_id={"row": me + 1}, device_id_type=MESH)

    inside = (me > 0) & (me < n - 1)

    @pl.when(inside)
    def _():
        pl.semaphore_wait(barrier, 2)

    @pl.when(jnp.logical_not(inside))
    def _():
        pl.semaphore_wait(barrier, 1)


def line_gather_kernel(n, own_ref, out_ref, send_right, recv_right, send_left, recv_left):
    me = lax.axis_index("row")
    greet_line(n, me)
    out_ref[me] = own_ref[...]

    def right(block, step, device):
        place = out_ref.at[block]
        return send(place, place, send_right.at[step], recv_right.at[step], {"row": device})

    def left(block, step, device):
        place = out_ref.at[block]
        return send(place, place, send_left.at[step], recv_left.at[step], {"row": device})

    for step in range(n - 1):

        @pl.when((me - step >= 0) & (me < n - 1))
        def _():
            right(me - step, step, me + 1).start()

        @pl.when((me + step < n) & (me > 0))
        def _():
            left(me + step, step, me - 1).start()

        @pl.when(me - 1 - step >= 0)
        def _():
            right(me - 1 - step, step, me - 1).wait_recv()

        @pl.when(me + 1 + step < n)
        def _():
            left(me + 1 + step, step, me + 1).wait_recv()

    for step in range(n - 1):

        @pl.when((me - step >= 0) & (me < n - 1))
        def _():
            right(me - step, step, me + 1).wait_send()

        @pl.when((me + step < n) & (me > 0))
        def _():
            left(me + step, step, me - 1).wait_send()


def line_gather(own, n, collective_id):
    rows, wide = own.shape
    return pl.pallas_call(
        functools.partial(line_gather_kernel, n),
        out_shape=jax.ShapeDtypeStruct((n, rows, wide), own.dtype),
        in_specs=[pl.BlockSpec(memory_space=pltpu.VMEM)],
        out_specs=pl.BlockSpec(memory_space=pltpu.VMEM),
        scratch_shapes=[pltpu.SemaphoreType.DMA((n - 1,))] * 4,
        compiler_params=pltpu.CompilerParams(
            collective_id=collective_id, has_side_effects=True, vmem_limit_bytes=32 * 2**20
        ),
    )(own).reshape(n * rows, wide)


def line_scatter_kernel(
    n, parts_ref, out_ref, from_left, from_right, send_right, recv_right, send_left, recv_left
):
    me = lax.axis_index("row")
    mirror = n - 1 - me
    greet_line(n, me)

    def target(step, place):
        return n - 1 - (step - place)

    def right(src, step, block, device):
        return send(
            src, from_left.at[block], send_right.at[step], recv_right.at[step], {"row": device}
        )

    def left(src, step, block, device):
        return send(
            src, from_right.at[block], send_left.at[step], recv_left.at[step], {"row": device}
        )

    for step in range(n - 1):
        block_right = target(step, me)
        block_left = n - 1 - target(step, mirror)
        sends_right = (step >= me) & (me < n - 1)
        sends_left = (step >= mirror) & (mirror < n - 1)

        @pl.when(sends_right & (me == 0))
        def _():
            right(parts_ref.at[block_right], step, block_right, me + 1).start()

        @pl.when(sends_right & (me > 0))
        def _():
            right(from_left.at[block_right], step, block_right, me + 1).start()

        @pl.when(sends_left & (mirror == 0))
        def _():
            left(parts_ref.at[block_left], step, block_left, me - 1).start()

        @pl.when(sends_left & (mirror > 0))
        def _():
            left(from_right.at[block_left], step, block_left, me - 1).start()

        coming_right = target(step, me - 1)
        coming_left = n - 1 - target(step, mirror - 1)

        @pl.when((me >= 1) & (step >= me - 1))
        def _():
            right(from_left.at[coming_right], step, coming_right, me - 1).wait_recv()

            @pl.when(coming_right > me)
            def _():
                from_left[coming_right] = from_left[coming_right] + parts_ref[coming_right]

        @pl.when((mirror >= 1) & (step >= mirror - 1))
        def _():
            left(from_right.at[coming_left], step, coming_left, me + 1).wait_recv()

            @pl.when(coming_left < me)
            def _():
                from_right[coming_left] = from_right[coming_left] + parts_ref[coming_left]

    out_ref[...] = parts_ref[me]

    @pl.when(me > 0)
    def _():
        out_ref[...] = out_ref[...] + from_left[me]

    @pl.when(mirror > 0)
    def _():
        out_ref[...] = out_ref[...] + from_right[me]

    for step in range(n - 1):
        block_right = target(step, me)
        block_left = n - 1 - target(step, mirror)

        @pl.when((step >= me) & (me < n - 1))
        def _():
            right(from_left.at[block_right], step, block_right, me + 1).wait_send()

        @pl.when((step >= mirror) & (mirror < n - 1))
        def _():
            left(from_right.at[block_left], step, block_left, me - 1).wait_send()


def line_scatter(partial, n, collective_id):
    rows, wide = partial.shape[0] // n, partial.shape[1]
    return pl.pallas_call(
        functools.partial(line_scatter_kernel, n),
        out_shape=jax.ShapeDtypeStruct((rows, wide), partial.dtype),
        in_specs=[pl.BlockSpec(memory_space=pltpu.VMEM)],
        out_specs=pl.BlockSpec(memory_space=pltpu.VMEM),
        scratch_shapes=[pltpu.VMEM((n, rows, wide), partial.dtype)] * 2
        + [pltpu.SemaphoreType.DMA((n - 1,))] * 4,
        compiler_params=pltpu.CompilerParams(
            collective_id=collective_id, has_side_effects=True, vmem_limit_bytes=32 * 2**20
        ),
    )(partial.reshape(n, rows, wide))


def greet_plane(nx, col):
    core, x = col % 2, col // 2
    partner = x * 2 + 1 - core
    peers = [lax.rem(x + step, nx) * 2 + core for step in range(1, nx)]
    barrier = pltpu.get_barrier_semaphore()
    for device in [partner] + peers:
        pl.semaphore_signal(barrier, inc=1, device_id={"col": device}, device_id_type=MESH)
    pl.semaphore_wait(barrier, nx)
    return core, x, partner


def spread_plane(nx, core, x, partner, out_ref, send_peer, recv_peer, send_core, recv_core):
    copies = []
    own = out_ref.at[x, core]
    for step in range(1, nx):
        peer = lax.rem(x + step, nx) * 2 + core
        copies.append(
            send(own, own, send_peer.at[step - 1], recv_peer.at[step - 1], {"col": peer})
        )
        copies[-1].start()
    copies.append(send(own, own, send_core.at[0], recv_core.at[0], {"col": partner}))
    copies[-1].start()
    for step in range(1, nx):
        origin = lax.rem(x + nx - step, nx)
        place = out_ref.at[origin, core]
        send(
            place, place, send_peer.at[step - 1], recv_peer.at[step - 1], {"col": origin * 2 + core}
        ).wait_recv()
        copies.append(send(place, place, send_core.at[step], recv_core.at[step], {"col": partner}))
        copies[-1].start()
    for step in range(nx):
        place = out_ref.at[lax.rem(x + nx - step, nx), 1 - core]
        send(
            place, place, send_core.at[step], recv_core.at[step], {"col": partner}
        ).wait_recv()
    for copy in copies:
        copy.wait_send()


def plane_gather_kernel(nx, own_ref, out_ref, *sems):
    core, x, partner = greet_plane(nx, lax.axis_index("col"))
    out_ref[x, core] = own_ref[...]
    spread_plane(nx, core, x, partner, out_ref, *sems)


def plane_sems(nx):
    return [pltpu.SemaphoreType.DMA((max(nx - 1, 1),))] * 2 + [pltpu.SemaphoreType.DMA((nx,))] * 2


def plane_gather(own, n, collective_id):
    nx = n // 2
    rows, wide = own.shape
    return pl.pallas_call(
        functools.partial(plane_gather_kernel, nx),
        out_shape=jax.ShapeDtypeStruct((nx, 2, rows, wide), own.dtype),
        in_specs=[pl.BlockSpec(memory_space=pltpu.VMEM)],
        out_specs=pl.BlockSpec(memory_space=pltpu.VMEM),
        scratch_shapes=plane_sems(nx),
        compiler_params=pltpu.CompilerParams(
            collective_id=collective_id, has_side_effects=True, vmem_limit_bytes=32 * 2**20
        ),
    )(own).reshape(n * rows, wide)


def plane_sum_kernel(
    nx, parts_ref, weight_ref, out_ref, half, landed, s_half, r_half, s_land, r_land, *sems
):
    core, x, partner = greet_plane(nx, lax.axis_index("col"))
    copies = []
    order = [lax.rem(x + step, nx) for step in list(range(1, nx)) + [0]]
    for step, k in enumerate(order):
        copies.append(
            send(
                parts_ref.at[k, 1 - core],
                half.at[k],
                s_half.at[step],
                r_half.at[step],
                {"col": partner},
            )
        )
        copies[-1].start()
    for step, k in enumerate(order):
        copies[step].wait_recv()
        half[k] = half[k] + parts_ref[k, core]
        if step < nx - 1:
            copies.append(
                send(
                    half.at[k],
                    landed.at[step],
                    s_land.at[step],
                    r_land.at[step],
                    {"col": k * 2 + core},
                )
            )
            copies[-1].start()
    total = half[x]
    for step in range(nx - 1):
        copies[nx + step].wait_recv()
        total = total + landed[step]
    out_ref[x, core] = total * weight_ref[...]
    spread_plane(nx, core, x, partner, out_ref, *sems)
    for copy in copies:
        copy.wait_send()


def plane_sum(partial, weight, n, collective_id):
    nx = n // 2
    rows, wide = partial.shape[0] // n, partial.shape[1]
    return pl.pallas_call(
        functools.partial(plane_sum_kernel, nx),
        out_shape=jax.ShapeDtypeStruct((nx, 2, rows, wide), partial.dtype),
        in_specs=[pl.BlockSpec(memory_space=pltpu.VMEM)] * 2,
        out_specs=pl.BlockSpec(memory_space=pltpu.VMEM),
        scratch_shapes=[
            pltpu.VMEM((nx, rows, wide), partial.dtype),
            pltpu.VMEM((max(nx - 1, 1), rows, wide), partial.dtype),
        ]
        + [pltpu.SemaphoreType.DMA((nx,))] * 2
        + [pltpu.SemaphoreType.DMA((max(nx - 1, 1),))] * 2
        + plane_sems(nx),
        compiler_params=pltpu.CompilerParams(
            collective_id=collective_id, has_side_effects=True, vmem_limit_bytes=32 * 2**20
        ),
    )(partial.reshape(nx, 2, rows, wide), weight).reshape(n * rows, wide)


def local(series, vectors, damp_class, damp_levels, removed_blocks):
    n_row, n_col = lax.axis_size("row"), lax.axis_size("col")
    row_id = lax.axis_index("row")
    col_id = lax.axis_index("col")
    shard_rows, samples = series.shape
    wide = vectors.shape[1]
    classes = damp_levels.shape[0]
    order = shard_rows * n_row * n_col
    z_own = standardize(series)
    onehot = (damp_class[:, None] == jnp.arange(classes, dtype=jnp.int32)[None, :]).astype(
        jnp.float32
    )
    damping = jnp.sum(onehot * damp_levels[None, :], axis=1)
    weight_own = damping * damping
    z_rows = lax.all_gather(z_own, "col", axis=0, tiled=True)
    z_cols = line_gather(z_own, n_row, 0)
    tile_rows, tile_cols = z_rows.shape[0], z_cols.shape[0]
    blocks = removed_blocks.shape[0]
    block_size = order // blocks
    row_block = (row_id * tile_rows + jnp.arange(tile_rows, dtype=jnp.int32)) // block_size
    position = jnp.arange(tile_cols, dtype=jnp.int32)
    col_index = (position // shard_rows * n_col + col_id) * shard_rows + position % shard_rows
    col_block = col_index // block_size
    keep = (1 - removed_blocks).astype(jnp.bfloat16)
    row_hot = (row_block[:, None] == jnp.arange(blocks)[None, :]).astype(jnp.bfloat16)
    col_hot = (col_block[:, None] == jnp.arange(blocks)[None, :]).astype(jnp.bfloat16)
    keep_rows = jnp.dot(row_hot, keep, preferred_element_type=jnp.float32).astype(jnp.bfloat16)
    rows_high, rows_low = split(z_rows)
    cols_high, cols_low = split(z_cols * (sharpness / samples))
    scores = lax.dot_general(
        jnp.concatenate([rows_high, rows_low, rows_high], axis=1),
        jnp.concatenate([cols_high, cols_high, cols_low], axis=1),
        (((1,), (1,)), ((), ())),
        preferred_element_type=jnp.float32,
    )
    keep_full = lax.dot_general(
        keep_rows, col_hot, (((1,), (1,)), ((), ())), preferred_element_type=jnp.float32
    )
    t_high, t_low = split(jnp.tanh(scores) * keep_full)
    spectral_scale = 0.5 * order * jnp.mean(damp_levels * damp_levels)

    def multiply(dims, field, fine):
        high, low = split(field)
        dims = ((dims, (0,)), ((), ()))
        both = lax.dot_general(
            t_high,
            jnp.concatenate([high, low], axis=1),
            dims,
            preferred_element_type=jnp.float32,
        )
        out = both[:, :wide] + both[:, wide:]
        if fine:
            out = out + lax.dot_general(t_low, high, dims, preferred_element_type=jnp.float32)
        return out

    weight_wide = jnp.broadcast_to(weight_own[:, None], (shard_rows, wide))

    def normal_apply(field_cols, fine):
        product = multiply((1,), field_cols, fine[0])
        product = plane_sum(product, weight_wide, n_col, 2)
        returned = multiply((0,), product, fine[1])
        return line_scatter(returned, n_row, 3) / spectral_scale

    vectors_cols = lax.all_gather(vectors, "row", axis=0, tiled=True)
    first_term = normal_apply(vectors_cols, (True, False)) - vectors
    first_cols = line_gather(first_term, n_row, 1)
    return 2.0 * (normal_apply(first_cols, (False, True)) - first_term) - vectors


def solution(mesh):
    placed = (
        P(("ens", "row", "col"), None),
        P(("ens", "row", "col"), None),
        P(("ens", "row", "col")),
        P(),
        P("ens", None),
    )
    return jax.shard_map(
        local, mesh=mesh, in_specs=placed, out_specs=P(("ens", "row", "col"), None), check_vma=False
    )
```

```python
import functools

import jax
import jax.numpy as jnp
from jax import lax
from jax.experimental import pallas as pl
from jax.experimental.pallas import tpu as pltpu
from jax.sharding import PartitionSpec as P


sharpness = 12.0


def standardize(series):
    centered = series - jnp.mean(series, axis=1, keepdims=True)
    spread = jnp.mean(centered * centered, axis=1, keepdims=True)
    return centered * lax.rsqrt(spread + 1e-05)


def split(x):
    high = lax.reduce_precision(x, 8, 7)
    return high.astype(jnp.bfloat16), (x - high).astype(jnp.bfloat16)


MESH = pl.DeviceIdType.MESH


def send(src, dst, send_sem, recv_sem, device):
    return pltpu.make_async_remote_copy(
        src_ref=src,
        dst_ref=dst,
        send_sem=send_sem,
        recv_sem=recv_sem,
        device_id=device,
        device_id_type=MESH,
    )


def greet_line(n, me):
    barrier = pltpu.get_barrier_semaphore()

    @pl.when(me > 0)
    def _():
        pl.semaphore_signal(barrier, inc=1, device_id={"row": me - 1}, device_id_type=MESH)

    @pl.when(me < n - 1)
    def _():
        pl.semaphore_signal(barrier, inc=1, device_id={"row": me + 1}, device_id_type=MESH)

    inside = (me > 0) & (me < n - 1)

    @pl.when(inside)
    def _():
        pl.semaphore_wait(barrier, 2)

    @pl.when(jnp.logical_not(inside))
    def _():
        pl.semaphore_wait(barrier, 1)


def line_gather_kernel(n, own_ref, out_ref, send_right, recv_right, send_left, recv_left):
    me = lax.axis_index("row")
    greet_line(n, me)
    out_ref[me] = own_ref[...]

    def right(block, step, device):
        place = out_ref.at[block]
        return send(place, place, send_right.at[step], recv_right.at[step], {"row": device})

    def left(block, step, device):
        place = out_ref.at[block]
        return send(place, place, send_left.at[step], recv_left.at[step], {"row": device})

    for step in range(n - 1):

        @pl.when((me - step >= 0) & (me < n - 1))
        def _():
            right(me - step, step, me + 1).start()

        @pl.when((me + step < n) & (me > 0))
        def _():
            left(me + step, step, me - 1).start()

        @pl.when(me - 1 - step >= 0)
        def _():
            right(me - 1 - step, step, me - 1).wait_recv()

        @pl.when(me + 1 + step < n)
        def _():
            left(me + 1 + step, step, me + 1).wait_recv()

    for step in range(n - 1):

        @pl.when((me - step >= 0) & (me < n - 1))
        def _():
            right(me - step, step, me + 1).wait_send()

        @pl.when((me + step < n) & (me > 0))
        def _():
            left(me + step, step, me - 1).wait_send()


def line_gather(own, n, collective_id):
    rows, wide = own.shape
    return pl.pallas_call(
        functools.partial(line_gather_kernel, n),
        out_shape=jax.ShapeDtypeStruct((n, rows, wide), own.dtype),
        in_specs=[pl.BlockSpec(memory_space=pltpu.VMEM)],
        out_specs=pl.BlockSpec(memory_space=pltpu.VMEM),
        scratch_shapes=[pltpu.SemaphoreType.DMA((n - 1,))] * 4,
        compiler_params=pltpu.CompilerParams(
            collective_id=collective_id, has_side_effects=True, vmem_limit_bytes=32 * 2**20
        ),
    )(own).reshape(n * rows, wide)


def line_scatter_kernel(
    n, parts_ref, out_ref, from_left, from_right, send_right, recv_right, send_left, recv_left
):
    me = lax.axis_index("row")
    mirror = n - 1 - me
    greet_line(n, me)

    def target(step, place):
        return n - 1 - (step - place)

    def right(src, step, block, device):
        return send(
            src, from_left.at[block], send_right.at[step], recv_right.at[step], {"row": device}
        )

    def left(src, step, block, device):
        return send(
            src, from_right.at[block], send_left.at[step], recv_left.at[step], {"row": device}
        )

    for step in range(n - 1):
        block_right = target(step, me)
        block_left = n - 1 - target(step, mirror)
        sends_right = (step >= me) & (me < n - 1)
        sends_left = (step >= mirror) & (mirror < n - 1)

        @pl.when(sends_right & (me == 0))
        def _():
            right(parts_ref.at[block_right], step, block_right, me + 1).start()

        @pl.when(sends_right & (me > 0))
        def _():
            right(from_left.at[block_right], step, block_right, me + 1).start()

        @pl.when(sends_left & (mirror == 0))
        def _():
            left(parts_ref.at[block_left], step, block_left, me - 1).start()

        @pl.when(sends_left & (mirror > 0))
        def _():
            left(from_right.at[block_left], step, block_left, me - 1).start()

        coming_right = target(step, me - 1)
        coming_left = n - 1 - target(step, mirror - 1)

        @pl.when((me >= 1) & (step >= me - 1))
        def _():
            right(from_left.at[coming_right], step, coming_right, me - 1).wait_recv()

            @pl.when(coming_right > me)
            def _():
                from_left[coming_right] = from_left[coming_right] + parts_ref[coming_right]

        @pl.when((mirror >= 1) & (step >= mirror - 1))
        def _():
            left(from_right.at[coming_left], step, coming_left, me + 1).wait_recv()

            @pl.when(coming_left < me)
            def _():
                from_right[coming_left] = from_right[coming_left] + parts_ref[coming_left]

    out_ref[...] = parts_ref[me]

    @pl.when(me > 0)
    def _():
        out_ref[...] = out_ref[...] + from_left[me]

    @pl.when(mirror > 0)
    def _():
        out_ref[...] = out_ref[...] + from_right[me]

    for step in range(n - 1):
        block_right = target(step, me)
        block_left = n - 1 - target(step, mirror)

        @pl.when((step >= me) & (me < n - 1))
        def _():
            right(from_left.at[block_right], step, block_right, me + 1).wait_send()

        @pl.when((step >= mirror) & (mirror < n - 1))
        def _():
            left(from_right.at[block_left], step, block_left, me - 1).wait_send()


def line_scatter(partial, n, collective_id):
    rows, wide = partial.shape[0] // n, partial.shape[1]
    return pl.pallas_call(
        functools.partial(line_scatter_kernel, n),
        out_shape=jax.ShapeDtypeStruct((rows, wide), partial.dtype),
        in_specs=[pl.BlockSpec(memory_space=pltpu.VMEM)],
        out_specs=pl.BlockSpec(memory_space=pltpu.VMEM),
        scratch_shapes=[pltpu.VMEM((n, rows, wide), partial.dtype)] * 2
        + [pltpu.SemaphoreType.DMA((n - 1,))] * 4,
        compiler_params=pltpu.CompilerParams(
            collective_id=collective_id, has_side_effects=True, vmem_limit_bytes=32 * 2**20
        ),
    )(partial.reshape(n, rows, wide))


def greet_plane(nx, col):
    core, x = col % 2, col // 2
    partner = x * 2 + 1 - core
    peers = [lax.rem(x + step, nx) * 2 + core for step in range(1, nx)]
    barrier = pltpu.get_barrier_semaphore()
    for device in [partner] + peers:
        pl.semaphore_signal(barrier, inc=1, device_id={"col": device}, device_id_type=MESH)
    pl.semaphore_wait(barrier, nx)
    return core, x, partner


def spread_plane(nx, core, x, partner, out_ref, send_peer, recv_peer, send_core, recv_core):
    copies = []
    own = out_ref.at[x, core]
    for step in range(1, nx):
        peer = lax.rem(x + step, nx) * 2 + core
        copies.append(
            send(own, own, send_peer.at[step - 1], recv_peer.at[step - 1], {"col": peer})
        )
        copies[-1].start()
    copies.append(send(own, own, send_core.at[0], recv_core.at[0], {"col": partner}))
    copies[-1].start()
    for step in range(1, nx):
        origin = lax.rem(x + nx - step, nx)
        place = out_ref.at[origin, core]
        send(
            place, place, send_peer.at[step - 1], recv_peer.at[step - 1], {"col": origin * 2 + core}
        ).wait_recv()
        copies.append(send(place, place, send_core.at[step], recv_core.at[step], {"col": partner}))
        copies[-1].start()
    for step in range(nx):
        place = out_ref.at[lax.rem(x + nx - step, nx), 1 - core]
        send(
            place, place, send_core.at[step], recv_core.at[step], {"col": partner}
        ).wait_recv()
    for copy in copies:
        copy.wait_send()


def plane_gather_kernel(nx, own_ref, out_ref, *sems):
    core, x, partner = greet_plane(nx, lax.axis_index("col"))
    out_ref[x, core] = own_ref[...]
    spread_plane(nx, core, x, partner, out_ref, *sems)


def plane_sems(nx):
    return [pltpu.SemaphoreType.DMA((max(nx - 1, 1),))] * 2 + [pltpu.SemaphoreType.DMA((nx,))] * 2


def plane_gather(own, n, collective_id):
    nx = n // 2
    rows, wide = own.shape
    return pl.pallas_call(
        functools.partial(plane_gather_kernel, nx),
        out_shape=jax.ShapeDtypeStruct((nx, 2, rows, wide), own.dtype),
        in_specs=[pl.BlockSpec(memory_space=pltpu.VMEM)],
        out_specs=pl.BlockSpec(memory_space=pltpu.VMEM),
        scratch_shapes=plane_sems(nx),
        compiler_params=pltpu.CompilerParams(
            collective_id=collective_id, has_side_effects=True, vmem_limit_bytes=32 * 2**20
        ),
    )(own).reshape(n * rows, wide)


def plane_sum_kernel(
    nx, parts_ref, weight_ref, out_ref, half, landed, s_half, r_half, s_land, r_land, *sems
):
    core, x, partner = greet_plane(nx, lax.axis_index("col"))
    copies = []
    order = [lax.rem(x + step, nx) for step in list(range(1, nx)) + [0]]
    for step, k in enumerate(order):
        copies.append(
            send(
                parts_ref.at[k, 1 - core],
                half.at[k],
                s_half.at[step],
                r_half.at[step],
                {"col": partner},
            )
        )
        copies[-1].start()
    for step, k in enumerate(order):
        copies[step].wait_recv()
        half[k] = half[k] + parts_ref[k, core]
        if step < nx - 1:
            copies.append(
                send(
                    half.at[k],
                    landed.at[step],
                    s_land.at[step],
                    r_land.at[step],
                    {"col": k * 2 + core},
                )
            )
            copies[-1].start()
    total = half[x]
    for step in range(nx - 1):
        copies[nx + step].wait_recv()
        total = total + landed[step]
    out_ref[x, core] = total * weight_ref[...]
    spread_plane(nx, core, x, partner, out_ref, *sems)
    for copy in copies:
        copy.wait_send()


def plane_sum(partial, weight, n, collective_id):
    nx = n // 2
    rows, wide = partial.shape[0] // n, partial.shape[1]
    return pl.pallas_call(
        functools.partial(plane_sum_kernel, nx),
        out_shape=jax.ShapeDtypeStruct((nx, 2, rows, wide), partial.dtype),
        in_specs=[pl.BlockSpec(memory_space=pltpu.VMEM)] * 2,
        out_specs=pl.BlockSpec(memory_space=pltpu.VMEM),
        scratch_shapes=[
            pltpu.VMEM((nx, rows, wide), partial.dtype),
            pltpu.VMEM((max(nx - 1, 1), rows, wide), partial.dtype),
        ]
        + [pltpu.SemaphoreType.DMA((nx,))] * 2
        + [pltpu.SemaphoreType.DMA((max(nx - 1, 1),))] * 2
        + plane_sems(nx),
        compiler_params=pltpu.CompilerParams(
            collective_id=collective_id, has_side_effects=True, vmem_limit_bytes=32 * 2**20
        ),
    )(partial.reshape(nx, 2, rows, wide), weight).reshape(n * rows, wide)


def local(series, vectors, damp_class, damp_levels, removed_blocks):
    n_row, n_col = lax.axis_size("row"), lax.axis_size("col")
    row_id = lax.axis_index("row")
    col_id = lax.axis_index("col")
    shard_rows, samples = series.shape
    wide = vectors.shape[1]
    classes = damp_levels.shape[0]
    order = shard_rows * n_row * n_col
    z_own = standardize(series)
    onehot = (damp_class[:, None] == jnp.arange(classes, dtype=jnp.int32)[None, :]).astype(
        jnp.float32
    )
    damping = jnp.sum(onehot * damp_levels[None, :], axis=1)
    weight_own = damping * damping
    z_rows = lax.all_gather(z_own, "col", axis=0, tiled=True)
    z_cols = line_gather(z_own, n_row, 0)
    z_cols, vectors = lax.optimization_barrier((z_cols, vectors))
    tile_rows, tile_cols = z_rows.shape[0], z_cols.shape[0]
    blocks = removed_blocks.shape[0]
    block_size = order // blocks
    row_blocks = tile_rows // block_size
    position = jnp.arange(tile_cols, dtype=jnp.int32)
    col_index = (position // shard_rows * n_col + col_id) * shard_rows + position % shard_rows
    col_block = col_index // block_size
    keep_rows = 1.0 - lax.dynamic_slice_in_dim(
        removed_blocks, row_id * row_blocks, row_blocks, 0
    ).astype(jnp.float32)
    col_hot = (col_block[None, :] == jnp.arange(blocks, dtype=jnp.int32)[:, None]).astype(
        jnp.float32
    )
    keep_small = jnp.dot(
        keep_rows, col_hot, precision=lax.Precision.HIGHEST, preferred_element_type=jnp.float32
    )
    keep_full = jnp.broadcast_to(
        keep_small[:, None, :], (row_blocks, block_size, tile_cols)
    ).reshape(tile_rows, tile_cols)
    rows_high, rows_low = split(z_rows)
    cols_high, cols_low = split(z_cols * (sharpness / samples))
    scores = lax.dot_general(
        jnp.concatenate([rows_high, rows_low, rows_high], axis=1),
        jnp.concatenate([cols_high, cols_high, cols_low], axis=1),
        (((1,), (1,)), ((), ())),
        preferred_element_type=jnp.float32,
    )
    t_high, t_low = split(jnp.tanh(scores) * keep_full)
    spectral_scale = 0.5 * order * jnp.mean(damp_levels * damp_levels)

    def multiply(dims, field, fine):
        high, low = split(field)
        dims = ((dims, (0,)), ((), ()))
        both = lax.dot_general(
            t_high,
            jnp.concatenate([high, low], axis=1),
            dims,
            preferred_element_type=jnp.float32,
        )
        if fine:
            both = both + lax.dot_general(
                t_low,
                jnp.concatenate([high, low], axis=1),
                dims,
                preferred_element_type=jnp.float32,
            )
        out = both[:, :wide] + both[:, wide:]
        return out

    weight_wide = jnp.broadcast_to(weight_own[:, None], (shard_rows, wide))

    def normal_apply(field_cols, fine):
        product = multiply((1,), field_cols, fine[0])
        product = plane_sum(product, weight_wide, n_col, 2)
        returned = multiply((0,), product, fine[1])
        return line_scatter(returned, n_row, 3) / spectral_scale

    vectors_cols = lax.all_gather(vectors, "row", axis=0, tiled=True)
    first_term = normal_apply(vectors_cols, (True, False)) - vectors
    first_cols = line_gather(first_term, n_row, 1)
    return 2.0 * (normal_apply(first_cols, (False, True)) - first_term) - vectors


def solution(mesh):
    placed = (
        P(("ens", "row", "col"), None),
        P(("ens", "row", "col"), None),
        P(("ens", "row", "col")),
        P(),
        P("ens", None),
    )
    return jax.shard_map(
        local, mesh=mesh, in_specs=placed, out_specs=P(("ens", "row", "col"), None), check_vma=False
    )
```

```python
import functools

import jax
import jax.numpy as jnp
from jax import lax
from jax.experimental import pallas as pl
from jax.experimental.pallas import tpu as pltpu
from jax.sharding import PartitionSpec as P


sharpness = 12.0


def standardize(series):
    centered = series - jnp.mean(series, axis=1, keepdims=True)
    spread = jnp.mean(centered * centered, axis=1, keepdims=True)
    return centered * lax.rsqrt(spread + 1e-05)


def split(x):
    high = lax.reduce_precision(x, 8, 7)
    return high.astype(jnp.bfloat16), (x - high).astype(jnp.bfloat16)


MESH = pl.DeviceIdType.MESH


def send(src, dst, send_sem, recv_sem, device):
    return pltpu.make_async_remote_copy(
        src_ref=src,
        dst_ref=dst,
        send_sem=send_sem,
        recv_sem=recv_sem,
        device_id=device,
        device_id_type=MESH,
    )


def greet_line(n, me):
    barrier = pltpu.get_barrier_semaphore()

    @pl.when(me > 0)
    def _():
        pl.semaphore_signal(barrier, inc=1, device_id={"row": me - 1}, device_id_type=MESH)

    @pl.when(me < n - 1)
    def _():
        pl.semaphore_signal(barrier, inc=1, device_id={"row": me + 1}, device_id_type=MESH)

    inside = (me > 0) & (me < n - 1)

    @pl.when(inside)
    def _():
        pl.semaphore_wait(barrier, 2)

    @pl.when(jnp.logical_not(inside))
    def _():
        pl.semaphore_wait(barrier, 1)


def line_gather_kernel(n, own_ref, out_ref, send_right, recv_right, send_left, recv_left):
    me = lax.axis_index("row")
    greet_line(n, me)
    out_ref[me] = own_ref[...]

    def right(block, step, device):
        place = out_ref.at[block]
        return send(place, place, send_right.at[step], recv_right.at[step], {"row": device})

    def left(block, step, device):
        place = out_ref.at[block]
        return send(place, place, send_left.at[step], recv_left.at[step], {"row": device})

    for step in range(n - 1):

        @pl.when((me - step >= 0) & (me < n - 1))
        def _():
            right(me - step, step, me + 1).start()

        @pl.when((me + step < n) & (me > 0))
        def _():
            left(me + step, step, me - 1).start()

        @pl.when(me - 1 - step >= 0)
        def _():
            right(me - 1 - step, step, me - 1).wait_recv()

        @pl.when(me + 1 + step < n)
        def _():
            left(me + 1 + step, step, me + 1).wait_recv()

    for step in range(n - 1):

        @pl.when((me - step >= 0) & (me < n - 1))
        def _():
            right(me - step, step, me + 1).wait_send()

        @pl.when((me + step < n) & (me > 0))
        def _():
            left(me + step, step, me - 1).wait_send()


def line_gather(own, n, collective_id):
    rows, wide = own.shape
    return pl.pallas_call(
        functools.partial(line_gather_kernel, n),
        out_shape=jax.ShapeDtypeStruct((n, rows, wide), own.dtype),
        in_specs=[pl.BlockSpec(memory_space=pltpu.VMEM)],
        out_specs=pl.BlockSpec(memory_space=pltpu.VMEM),
        scratch_shapes=[pltpu.SemaphoreType.DMA((n - 1,))] * 4,
        compiler_params=pltpu.CompilerParams(
            collective_id=collective_id, has_side_effects=True, vmem_limit_bytes=32 * 2**20
        ),
    )(own).reshape(n * rows, wide)


def cross_gather_kernel(
    n, nx, own_ref, cols_ref, rows_ref, send_right, recv_right, send_left, recv_left, *sems
):
    send_peer, recv_peer, send_core, recv_core = sems
    me, col = lax.axis_index("row"), lax.axis_index("col")
    core, x = col % 2, col // 2
    partner = x * 2 + 1 - core
    peers = [lax.rem(x + step, nx) * 2 + core for step in range(1, nx)]
    barrier = pltpu.get_barrier_semaphore()
    for device in [partner] + peers:
        pl.semaphore_signal(barrier, inc=1, device_id={"col": device}, device_id_type=MESH)

    @pl.when(me > 0)
    def _():
        pl.semaphore_signal(barrier, inc=1, device_id={"row": me - 1}, device_id_type=MESH)

    @pl.when(me < n - 1)
    def _():
        pl.semaphore_signal(barrier, inc=1, device_id={"row": me + 1}, device_id_type=MESH)

    inside = (me > 0) & (me < n - 1)

    @pl.when(inside)
    def _():
        pl.semaphore_wait(barrier, nx + 2)

    @pl.when(jnp.logical_not(inside))
    def _():
        pl.semaphore_wait(barrier, nx + 1)

    cols_ref[me] = own_ref[...]
    rows_ref[x, core] = own_ref[...]

    def right(block, step, device):
        place = cols_ref.at[block]
        return send(place, place, send_right.at[step], recv_right.at[step], {"row": device})

    def left(block, step, device):
        place = cols_ref.at[block]
        return send(place, place, send_left.at[step], recv_left.at[step], {"row": device})

    copies = []
    for step in range(n - 1):

        @pl.when((me - step >= 0) & (me < n - 1))
        def _():
            right(me - step, step, me + 1).start()

        @pl.when((me + step < n) & (me > 0))
        def _():
            left(me + step, step, me - 1).start()

        if step == 0:
            own = rows_ref.at[x, core]
            for hop in range(1, nx):
                copies.append(
                    send(
                        own,
                        own,
                        send_peer.at[hop - 1],
                        recv_peer.at[hop - 1],
                        {"col": peers[hop - 1]},
                    )
                )
                copies[-1].start()
            copies.append(send(own, own, send_core.at[0], recv_core.at[0], {"col": partner}))
            copies[-1].start()

        @pl.when(me - 1 - step >= 0)
        def _():
            right(me - 1 - step, step, me - 1).wait_recv()

        @pl.when(me + 1 + step < n)
        def _():
            left(me + 1 + step, step, me + 1).wait_recv()

    for hop in range(1, nx):
        origin = lax.rem(x + nx - hop, nx)
        place = rows_ref.at[origin, core]
        send(
            place, place, send_peer.at[hop - 1], recv_peer.at[hop - 1], {"col": origin * 2 + core}
        ).wait_recv()
        copies.append(send(place, place, send_core.at[hop], recv_core.at[hop], {"col": partner}))
        copies[-1].start()
    for hop in range(nx):
        place = rows_ref.at[lax.rem(x + nx - hop, nx), 1 - core]
        send(place, place, send_core.at[hop], recv_core.at[hop], {"col": partner}).wait_recv()
    for copy in copies:
        copy.wait_send()
    for step in range(n - 1):

        @pl.when((me - step >= 0) & (me < n - 1))
        def _():
            right(me - step, step, me + 1).wait_send()

        @pl.when((me + step < n) & (me > 0))
        def _():
            left(me + step, step, me - 1).wait_send()


def cross_gather(own, n, n_col, collective_id):
    nx = n_col // 2
    rows, wide = own.shape
    by_row, by_col = pl.pallas_call(
        functools.partial(cross_gather_kernel, n, nx),
        out_shape=(
            jax.ShapeDtypeStruct((n, rows, wide), own.dtype),
            jax.ShapeDtypeStruct((nx, 2, rows, wide), own.dtype),
        ),
        in_specs=[pl.BlockSpec(memory_space=pltpu.VMEM)],
        out_specs=(
            pl.BlockSpec(memory_space=pltpu.VMEM),
            pl.BlockSpec(memory_space=pltpu.VMEM),
        ),
        scratch_shapes=[pltpu.SemaphoreType.DMA((n - 1,))] * 4 + plane_sems(nx),
        compiler_params=pltpu.CompilerParams(
            collective_id=collective_id, has_side_effects=True, vmem_limit_bytes=32 * 2**20
        ),
    )(own)
    return by_row.reshape(n * rows, wide), by_col.reshape(n_col * rows, wide)


def line_scatter_kernel(
    n, parts_ref, out_ref, from_left, from_right, send_right, recv_right, send_left, recv_left
):
    me = lax.axis_index("row")
    mirror = n - 1 - me
    greet_line(n, me)

    def target(step, place):
        return n - 1 - (step - place)

    def right(src, step, block, device):
        return send(
            src, from_left.at[block], send_right.at[step], recv_right.at[step], {"row": device}
        )

    def left(src, step, block, device):
        return send(
            src, from_right.at[block], send_left.at[step], recv_left.at[step], {"row": device}
        )

    for step in range(n - 1):
        block_right = target(step, me)
        block_left = n - 1 - target(step, mirror)
        sends_right = (step >= me) & (me < n - 1)
        sends_left = (step >= mirror) & (mirror < n - 1)

        @pl.when(sends_right & (me == 0))
        def _():
            right(parts_ref.at[block_right], step, block_right, me + 1).start()

        @pl.when(sends_right & (me > 0))
        def _():
            right(from_left.at[block_right], step, block_right, me + 1).start()

        @pl.when(sends_left & (mirror == 0))
        def _():
            left(parts_ref.at[block_left], step, block_left, me - 1).start()

        @pl.when(sends_left & (mirror > 0))
        def _():
            left(from_right.at[block_left], step, block_left, me - 1).start()

        coming_right = target(step, me - 1)
        coming_left = n - 1 - target(step, mirror - 1)

        @pl.when((me >= 1) & (step >= me - 1))
        def _():
            right(from_left.at[coming_right], step, coming_right, me - 1).wait_recv()

            @pl.when(coming_right > me)
            def _():
                from_left[coming_right] = from_left[coming_right] + parts_ref[coming_right]

        @pl.when((mirror >= 1) & (step >= mirror - 1))
        def _():
            left(from_right.at[coming_left], step, coming_left, me + 1).wait_recv()

            @pl.when(coming_left < me)
            def _():
                from_right[coming_left] = from_right[coming_left] + parts_ref[coming_left]

    out_ref[...] = parts_ref[me]

    @pl.when(me > 0)
    def _():
        out_ref[...] = out_ref[...] + from_left[me]

    @pl.when(mirror > 0)
    def _():
        out_ref[...] = out_ref[...] + from_right[me]

    for step in range(n - 1):
        block_right = target(step, me)
        block_left = n - 1 - target(step, mirror)

        @pl.when((step >= me) & (me < n - 1))
        def _():
            right(from_left.at[block_right], step, block_right, me + 1).wait_send()

        @pl.when((step >= mirror) & (mirror < n - 1))
        def _():
            left(from_right.at[block_left], step, block_left, me - 1).wait_send()


def line_scatter(partial, n, collective_id):
    rows, wide = partial.shape[0] // n, partial.shape[1]
    return pl.pallas_call(
        functools.partial(line_scatter_kernel, n),
        out_shape=jax.ShapeDtypeStruct((rows, wide), partial.dtype),
        in_specs=[pl.BlockSpec(memory_space=pltpu.VMEM)],
        out_specs=pl.BlockSpec(memory_space=pltpu.VMEM),
        scratch_shapes=[pltpu.VMEM((n, rows, wide), partial.dtype)] * 2
        + [pltpu.SemaphoreType.DMA((n - 1,))] * 4,
        compiler_params=pltpu.CompilerParams(
            collective_id=collective_id, has_side_effects=True, vmem_limit_bytes=32 * 2**20
        ),
    )(partial.reshape(n, rows, wide))


def greet_plane(nx, col):
    core, x = col % 2, col // 2
    partner = x * 2 + 1 - core
    peers = [lax.rem(x + step, nx) * 2 + core for step in range(1, nx)]
    barrier = pltpu.get_barrier_semaphore()
    for device in [partner] + peers:
        pl.semaphore_signal(barrier, inc=1, device_id={"col": device}, device_id_type=MESH)
    pl.semaphore_wait(barrier, nx)
    return core, x, partner


def spread_plane(nx, core, x, partner, out_ref, send_peer, recv_peer, send_core, recv_core):
    copies = []
    own = out_ref.at[x, core]
    for step in range(1, nx):
        peer = lax.rem(x + step, nx) * 2 + core
        copies.append(
            send(own, own, send_peer.at[step - 1], recv_peer.at[step - 1], {"col": peer})
        )
        copies[-1].start()
    copies.append(send(own, own, send_core.at[0], recv_core.at[0], {"col": partner}))
    copies[-1].start()
    for step in range(1, nx):
        origin = lax.rem(x + nx - step, nx)
        place = out_ref.at[origin, core]
        send(
            place, place, send_peer.at[step - 1], recv_peer.at[step - 1], {"col": origin * 2 + core}
        ).wait_recv()
        copies.append(send(place, place, send_core.at[step], recv_core.at[step], {"col": partner}))
        copies[-1].start()
    for step in range(nx):
        place = out_ref.at[lax.rem(x + nx - step, nx), 1 - core]
        send(
            place, place, send_core.at[step], recv_core.at[step], {"col": partner}
        ).wait_recv()
    for copy in copies:
        copy.wait_send()


def plane_gather_kernel(nx, own_ref, out_ref, *sems):
    core, x, partner = greet_plane(nx, lax.axis_index("col"))
    out_ref[x, core] = own_ref[...]
    spread_plane(nx, core, x, partner, out_ref, *sems)


def plane_sems(nx):
    return [pltpu.SemaphoreType.DMA((max(nx - 1, 1),))] * 2 + [pltpu.SemaphoreType.DMA((nx,))] * 2


def plane_gather(own, n, collective_id):
    nx = n // 2
    rows, wide = own.shape
    return pl.pallas_call(
        functools.partial(plane_gather_kernel, nx),
        out_shape=jax.ShapeDtypeStruct((nx, 2, rows, wide), own.dtype),
        in_specs=[pl.BlockSpec(memory_space=pltpu.VMEM)],
        out_specs=pl.BlockSpec(memory_space=pltpu.VMEM),
        scratch_shapes=plane_sems(nx),
        compiler_params=pltpu.CompilerParams(
            collective_id=collective_id, has_side_effects=True, vmem_limit_bytes=32 * 2**20
        ),
    )(own).reshape(n * rows, wide)


def plane_sum_kernel(
    nx, parts_ref, weight_ref, out_ref, half, landed, s_half, r_half, s_land, r_land, *sems
):
    core, x, partner = greet_plane(nx, lax.axis_index("col"))
    copies = []
    order = [lax.rem(x + step, nx) for step in list(range(1, nx)) + [0]]
    for step, k in enumerate(order):
        copies.append(
            send(
                parts_ref.at[k, 1 - core],
                half.at[k],
                s_half.at[step],
                r_half.at[step],
                {"col": partner},
            )
        )
        copies[-1].start()
    for step, k in enumerate(order):
        copies[step].wait_recv()
        half[k] = half[k] + parts_ref[k, core]
        if step < nx - 1:
            copies.append(
                send(
                    half.at[k],
                    landed.at[step],
                    s_land.at[step],
                    r_land.at[step],
                    {"col": k * 2 + core},
                )
            )
            copies[-1].start()
    total = half[x]
    for step in range(nx - 1):
        copies[nx + step].wait_recv()
        total = total + landed[step]
    out_ref[x, core] = total * weight_ref[...]
    spread_plane(nx, core, x, partner, out_ref, *sems)
    for copy in copies:
        copy.wait_send()


def plane_sum(partial, weight, n, collective_id):
    nx = n // 2
    rows, wide = partial.shape[0] // n, partial.shape[1]
    return pl.pallas_call(
        functools.partial(plane_sum_kernel, nx),
        out_shape=jax.ShapeDtypeStruct((nx, 2, rows, wide), partial.dtype),
        in_specs=[pl.BlockSpec(memory_space=pltpu.VMEM)] * 2,
        out_specs=pl.BlockSpec(memory_space=pltpu.VMEM),
        scratch_shapes=[
            pltpu.VMEM((nx, rows, wide), partial.dtype),
            pltpu.VMEM((max(nx - 1, 1), rows, wide), partial.dtype),
        ]
        + [pltpu.SemaphoreType.DMA((nx,))] * 2
        + [pltpu.SemaphoreType.DMA((max(nx - 1, 1),))] * 2
        + plane_sems(nx),
        compiler_params=pltpu.CompilerParams(
            collective_id=collective_id, has_side_effects=True, vmem_limit_bytes=32 * 2**20
        ),
    )(partial.reshape(nx, 2, rows, wide), weight).reshape(n * rows, wide)


def local(series, vectors, damp_class, damp_levels, removed_blocks):
    n_row, n_col = lax.axis_size("row"), lax.axis_size("col")
    row_id = lax.axis_index("row")
    col_id = lax.axis_index("col")
    shard_rows, samples = series.shape
    wide = vectors.shape[1]
    classes = damp_levels.shape[0]
    order = shard_rows * n_row * n_col
    z_own = standardize(series)
    onehot = (damp_class[:, None] == jnp.arange(classes, dtype=jnp.int32)[None, :]).astype(
        jnp.float32
    )
    damping = jnp.sum(onehot * damp_levels[None, :], axis=1)
    weight_own = damping * damping
    z_cols, z_rows = cross_gather(z_own, n_row, n_col, 0)
    z_cols, vectors = lax.optimization_barrier((z_cols, vectors))
    tile_rows, tile_cols = z_rows.shape[0], z_cols.shape[0]
    blocks = removed_blocks.shape[0]
    block_size = order // blocks
    row_blocks = tile_rows // block_size
    position = jnp.arange(tile_cols, dtype=jnp.int32)
    col_index = (position // shard_rows * n_col + col_id) * shard_rows + position % shard_rows
    col_block = col_index // block_size
    keep_rows = 1.0 - lax.dynamic_slice_in_dim(
        removed_blocks, row_id * row_blocks, row_blocks, 0
    ).astype(jnp.float32)
    col_hot = (col_block[None, :] == jnp.arange(blocks, dtype=jnp.int32)[:, None]).astype(
        jnp.float32
    )
    keep_small = jnp.dot(
        keep_rows, col_hot, precision=lax.Precision.HIGHEST, preferred_element_type=jnp.float32
    )
    keep_full = jnp.broadcast_to(
        keep_small[:, None, :], (row_blocks, block_size, tile_cols)
    ).reshape(tile_rows, tile_cols)
    rows_high, rows_low = split(z_rows)
    cols_high, cols_low = split(z_cols * (sharpness / samples))
    scores = lax.dot_general(
        jnp.concatenate([rows_high, rows_low, rows_high], axis=1),
        jnp.concatenate([cols_high, cols_high, cols_low], axis=1),
        (((1,), (1,)), ((), ())),
        preferred_element_type=jnp.float32,
    )
    t_high, t_low = split(jnp.tanh(scores) * keep_full)
    spectral_scale = 0.5 * order * jnp.mean(damp_levels * damp_levels)

    def multiply(dims, field, fine):
        high, low = split(field)
        dims = ((dims, (0,)), ((), ()))
        both = lax.dot_general(
            t_high,
            jnp.concatenate([high, low], axis=1),
            dims,
            preferred_element_type=jnp.float32,
        )
        if fine:
            both = both + lax.dot_general(
                t_low,
                jnp.concatenate([high, low], axis=1),
                dims,
                preferred_element_type=jnp.float32,
            )
        out = both[:, :wide] + both[:, wide:]
        return out

    weight_wide = jnp.broadcast_to(weight_own[:, None], (shard_rows, wide))

    def normal_apply(field_cols, fine):
        product = multiply((1,), field_cols, fine[0])
        product = plane_sum(product, weight_wide, n_col, 2)
        returned = multiply((0,), product, fine[1])
        return line_scatter(returned, n_row, 3) / spectral_scale

    vectors_cols = lax.all_gather(vectors, "row", axis=0, tiled=True)
    vectors_cols, t_high, t_low = lax.optimization_barrier((vectors_cols, t_high, t_low))
    first_term = normal_apply(vectors_cols, (True, False)) - vectors
    first_cols = line_gather(first_term, n_row, 1)
    return 2.0 * (normal_apply(first_cols, (False, True)) - first_term) - vectors


def solution(mesh):
    placed = (
        P(("ens", "row", "col"), None),
        P(("ens", "row", "col"), None),
        P(("ens", "row", "col")),
        P(),
        P("ens", None),
    )
    return jax.shard_map(
        local, mesh=mesh, in_specs=placed, out_specs=P(("ens", "row", "col"), None), check_vma=False
    )
```

```python
import functools

import jax
import jax.numpy as jnp
from jax import lax
from jax.experimental import pallas as pl
from jax.experimental.pallas import tpu as pltpu
from jax.sharding import PartitionSpec as P


sharpness = 12.0


def standardize(series):
    centered = series - jnp.mean(series, axis=1, keepdims=True)
    spread = jnp.mean(centered * centered, axis=1, keepdims=True)
    return centered * lax.rsqrt(spread + 1e-05)


def split(x):
    high = lax.reduce_precision(x, 8, 7)
    return high.astype(jnp.bfloat16), (x - high).astype(jnp.bfloat16)


MESH = pl.DeviceIdType.MESH


def send(src, dst, send_sem, recv_sem, device):
    return pltpu.make_async_remote_copy(
        src_ref=src,
        dst_ref=dst,
        send_sem=send_sem,
        recv_sem=recv_sem,
        device_id=device,
        device_id_type=MESH,
    )


def greet_line(n, me):
    barrier = pltpu.get_barrier_semaphore()

    @pl.when(me > 0)
    def _():
        pl.semaphore_signal(barrier, inc=1, device_id={"row": me - 1}, device_id_type=MESH)

    @pl.when(me < n - 1)
    def _():
        pl.semaphore_signal(barrier, inc=1, device_id={"row": me + 1}, device_id_type=MESH)

    inside = (me > 0) & (me < n - 1)

    @pl.when(inside)
    def _():
        pl.semaphore_wait(barrier, 2)

    @pl.when(jnp.logical_not(inside))
    def _():
        pl.semaphore_wait(barrier, 1)


def line_gather_kernel(n, own_ref, out_ref, send_right, recv_right, send_left, recv_left):
    me = lax.axis_index("row")
    greet_line(n, me)
    out_ref[me] = own_ref[...]

    def right(block, step, device):
        half = out_ref.shape[1] // 2
        place = out_ref.at[block, pl.ds(step % 2 * half, half)]
        return send(place, place, send_right.at[step], recv_right.at[step], {"row": device})

    def left(block, step, device):
        half = out_ref.shape[1] // 2
        place = out_ref.at[block, pl.ds(step % 2 * half, half)]
        return send(place, place, send_left.at[step], recv_left.at[step], {"row": device})

    for step in range(2 * n - 2):

        if step >= 2:
            done = step - 2
            @pl.when(me - 1 - done // 2 >= 0)
            def _():
                right(me - 1 - done // 2, done, me - 1).wait_recv()

            @pl.when(me + 1 + done // 2 < n)
            def _():
                left(me + 1 + done // 2, done, me + 1).wait_recv()

        @pl.when((me - step // 2 >= 0) & (me < n - 1))
        def _():
            right(me - step // 2, step, me + 1).start()

        @pl.when((me + step // 2 < n) & (me > 0))
        def _():
            left(me + step // 2, step, me - 1).start()

    for done in range(2 * n - 4, 2 * n - 2):

        @pl.when(me - 1 - done // 2 >= 0)
        def _():
            right(me - 1 - done // 2, done, me - 1).wait_recv()

        @pl.when(me + 1 + done // 2 < n)
        def _():
            left(me + 1 + done // 2, done, me + 1).wait_recv()

    for step in range(2 * n - 2):

        @pl.when((me - step // 2 >= 0) & (me < n - 1))
        def _():
            right(me - step // 2, step, me + 1).wait_send()

        @pl.when((me + step // 2 < n) & (me > 0))
        def _():
            left(me + step // 2, step, me - 1).wait_send()


def line_gather(own, n, collective_id):
    rows, wide = own.shape
    return pl.pallas_call(
        functools.partial(line_gather_kernel, n),
        out_shape=jax.ShapeDtypeStruct((n, rows, wide), own.dtype),
        in_specs=[pl.BlockSpec(memory_space=pltpu.VMEM)],
        out_specs=pl.BlockSpec(memory_space=pltpu.VMEM),
        scratch_shapes=[pltpu.SemaphoreType.DMA((2 * n - 2,))] * 4,
        compiler_params=pltpu.CompilerParams(
            collective_id=collective_id, has_side_effects=True, vmem_limit_bytes=32 * 2**20
        ),
    )(own).reshape(n * rows, wide)


def cross_gather_kernel(
    n, nx, own_ref, cols_ref, rows_ref, send_right, recv_right, send_left, recv_left, *sems
):
    send_peer, recv_peer, send_core, recv_core = sems
    me, col = lax.axis_index("row"), lax.axis_index("col")
    core, x = col % 2, col // 2
    partner = x * 2 + 1 - core
    peers = [lax.rem(x + step, nx) * 2 + core for step in range(1, nx)]
    barrier = pltpu.get_barrier_semaphore()
    for device in [partner] + peers:
        pl.semaphore_signal(barrier, inc=1, device_id={"col": device}, device_id_type=MESH)

    @pl.when(me > 0)
    def _():
        pl.semaphore_signal(barrier, inc=1, device_id={"row": me - 1}, device_id_type=MESH)

    @pl.when(me < n - 1)
    def _():
        pl.semaphore_signal(barrier, inc=1, device_id={"row": me + 1}, device_id_type=MESH)

    inside = (me > 0) & (me < n - 1)

    @pl.when(inside)
    def _():
        pl.semaphore_wait(barrier, nx + 2)

    @pl.when(jnp.logical_not(inside))
    def _():
        pl.semaphore_wait(barrier, nx + 1)

    cols_ref[me] = own_ref[...]
    rows_ref[x, core] = own_ref[...]

    def right(block, step, device):
        half = cols_ref.shape[1] // 2
        place = cols_ref.at[block, pl.ds(step % 2 * half, half)]
        return send(place, place, send_right.at[step], recv_right.at[step], {"row": device})

    def left(block, step, device):
        half = cols_ref.shape[1] // 2
        place = cols_ref.at[block, pl.ds(step % 2 * half, half)]
        return send(place, place, send_left.at[step], recv_left.at[step], {"row": device})

    copies = []
    for step in range(2 * n - 2):

        if step >= 2:
            done = step - 2
            @pl.when(me - 1 - done // 2 >= 0)
            def _():
                right(me - 1 - done // 2, done, me - 1).wait_recv()

            @pl.when(me + 1 + done // 2 < n)
            def _():
                left(me + 1 + done // 2, done, me + 1).wait_recv()

        @pl.when((me - step // 2 >= 0) & (me < n - 1))
        def _():
            right(me - step // 2, step, me + 1).start()

        @pl.when((me + step // 2 < n) & (me > 0))
        def _():
            left(me + step // 2, step, me - 1).start()

        if step == 0:
            own = rows_ref.at[x, core]
            for hop in range(1, nx):
                copies.append(
                    send(
                        own,
                        own,
                        send_peer.at[hop - 1],
                        recv_peer.at[hop - 1],
                        {"col": peers[hop - 1]},
                    )
                )
                copies[-1].start()
            copies.append(send(own, own, send_core.at[0], recv_core.at[0], {"col": partner}))
            copies[-1].start()

    for done in range(2 * n - 4, 2 * n - 2):

        @pl.when(me - 1 - done // 2 >= 0)
        def _():
            right(me - 1 - done // 2, done, me - 1).wait_recv()

        @pl.when(me + 1 + done // 2 < n)
        def _():
            left(me + 1 + done // 2, done, me + 1).wait_recv()

    for hop in range(1, nx):
        origin = lax.rem(x + nx - hop, nx)
        place = rows_ref.at[origin, core]
        send(
            place, place, send_peer.at[hop - 1], recv_peer.at[hop - 1], {"col": origin * 2 + core}
        ).wait_recv()
        copies.append(send(place, place, send_core.at[hop], recv_core.at[hop], {"col": partner}))
        copies[-1].start()
    for hop in range(nx):
        place = rows_ref.at[lax.rem(x + nx - hop, nx), 1 - core]
        send(place, place, send_core.at[hop], recv_core.at[hop], {"col": partner}).wait_recv()
    for copy in copies:
        copy.wait_send()
    for step in range(2 * n - 2):

        @pl.when((me - step // 2 >= 0) & (me < n - 1))
        def _():
            right(me - step // 2, step, me + 1).wait_send()

        @pl.when((me + step // 2 < n) & (me > 0))
        def _():
            left(me + step // 2, step, me - 1).wait_send()


def cross_gather(own, n, n_col, collective_id):
    nx = n_col // 2
    rows, wide = own.shape
    by_row, by_col = pl.pallas_call(
        functools.partial(cross_gather_kernel, n, nx),
        out_shape=(
            jax.ShapeDtypeStruct((n, rows, wide), own.dtype),
            jax.ShapeDtypeStruct((nx, 2, rows, wide), own.dtype),
        ),
        in_specs=[pl.BlockSpec(memory_space=pltpu.VMEM)],
        out_specs=(
            pl.BlockSpec(memory_space=pltpu.VMEM),
            pl.BlockSpec(memory_space=pltpu.VMEM),
        ),
        scratch_shapes=[pltpu.SemaphoreType.DMA((2 * n - 2,))] * 4 + plane_sems(nx),
        compiler_params=pltpu.CompilerParams(
            collective_id=collective_id, has_side_effects=True, vmem_limit_bytes=32 * 2**20
        ),
    )(own)
    return by_row.reshape(n * rows, wide), by_col.reshape(n_col * rows, wide)


def line_scatter_kernel(
    n, parts_ref, out_ref, from_left, from_right, send_right, recv_right, send_left, recv_left
):
    me = lax.axis_index("row")
    mirror = n - 1 - me
    greet_line(n, me)

    def target(step, place):
        return n - 1 - (step - place)

    def right(src, step, block, device):
        return send(
            src, from_left.at[block], send_right.at[step], recv_right.at[step], {"row": device}
        )

    def left(src, step, block, device):
        return send(
            src, from_right.at[block], send_left.at[step], recv_left.at[step], {"row": device}
        )

    for step in range(n - 1):
        block_right = target(step, me)
        block_left = n - 1 - target(step, mirror)
        sends_right = (step >= me) & (me < n - 1)
        sends_left = (step >= mirror) & (mirror < n - 1)

        @pl.when(sends_right & (me == 0))
        def _():
            right(parts_ref.at[block_right], step, block_right, me + 1).start()

        @pl.when(sends_right & (me > 0))
        def _():
            right(from_left.at[block_right], step, block_right, me + 1).start()

        @pl.when(sends_left & (mirror == 0))
        def _():
            left(parts_ref.at[block_left], step, block_left, me - 1).start()

        @pl.when(sends_left & (mirror > 0))
        def _():
            left(from_right.at[block_left], step, block_left, me - 1).start()

        coming_right = target(step, me - 1)
        coming_left = n - 1 - target(step, mirror - 1)

        @pl.when((me >= 1) & (step >= me - 1))
        def _():
            right(from_left.at[coming_right], step, coming_right, me - 1).wait_recv()

            @pl.when(coming_right > me)
            def _():
                from_left[coming_right] = from_left[coming_right] + parts_ref[coming_right]

        @pl.when((mirror >= 1) & (step >= mirror - 1))
        def _():
            left(from_right.at[coming_left], step, coming_left, me + 1).wait_recv()

            @pl.when(coming_left < me)
            def _():
                from_right[coming_left] = from_right[coming_left] + parts_ref[coming_left]

    out_ref[...] = parts_ref[me]

    @pl.when(me > 0)
    def _():
        out_ref[...] = out_ref[...] + from_left[me]

    @pl.when(mirror > 0)
    def _():
        out_ref[...] = out_ref[...] + from_right[me]

    for step in range(n - 1):
        block_right = target(step, me)
        block_left = n - 1 - target(step, mirror)

        @pl.when((step >= me) & (me < n - 1))
        def _():
            right(from_left.at[block_right], step, block_right, me + 1).wait_send()

        @pl.when((step >= mirror) & (mirror < n - 1))
        def _():
            left(from_right.at[block_left], step, block_left, me - 1).wait_send()


def line_scatter(partial, n, collective_id):
    rows, wide = partial.shape[0] // n, partial.shape[1]
    return pl.pallas_call(
        functools.partial(line_scatter_kernel, n),
        out_shape=jax.ShapeDtypeStruct((rows, wide), partial.dtype),
        in_specs=[pl.BlockSpec(memory_space=pltpu.VMEM)],
        out_specs=pl.BlockSpec(memory_space=pltpu.VMEM),
        scratch_shapes=[pltpu.VMEM((n, rows, wide), partial.dtype)] * 2
        + [pltpu.SemaphoreType.DMA((n - 1,))] * 4,
        compiler_params=pltpu.CompilerParams(
            collective_id=collective_id, has_side_effects=True, vmem_limit_bytes=32 * 2**20
        ),
    )(partial.reshape(n, rows, wide))


def greet_plane(nx, col):
    core, x = col % 2, col // 2
    partner = x * 2 + 1 - core
    peers = [lax.rem(x + step, nx) * 2 + core for step in range(1, nx)]
    barrier = pltpu.get_barrier_semaphore()
    for device in [partner] + peers:
        pl.semaphore_signal(barrier, inc=1, device_id={"col": device}, device_id_type=MESH)
    pl.semaphore_wait(barrier, nx)
    return core, x, partner


def spread_plane(nx, core, x, partner, out_ref, send_peer, recv_peer, send_core, recv_core):
    copies = []
    own = out_ref.at[x, core]
    for step in range(1, nx):
        peer = lax.rem(x + step, nx) * 2 + core
        copies.append(
            send(own, own, send_peer.at[step - 1], recv_peer.at[step - 1], {"col": peer})
        )
        copies[-1].start()
    copies.append(send(own, own, send_core.at[0], recv_core.at[0], {"col": partner}))
    copies[-1].start()
    for step in range(1, nx):
        origin = lax.rem(x + nx - step, nx)
        place = out_ref.at[origin, core]
        send(
            place, place, send_peer.at[step - 1], recv_peer.at[step - 1], {"col": origin * 2 + core}
        ).wait_recv()
        copies.append(send(place, place, send_core.at[step], recv_core.at[step], {"col": partner}))
        copies[-1].start()
    for step in range(nx):
        place = out_ref.at[lax.rem(x + nx - step, nx), 1 - core]
        send(
            place, place, send_core.at[step], recv_core.at[step], {"col": partner}
        ).wait_recv()
    for copy in copies:
        copy.wait_send()


def plane_gather_kernel(nx, own_ref, out_ref, *sems):
    core, x, partner = greet_plane(nx, lax.axis_index("col"))
    out_ref[x, core] = own_ref[...]
    spread_plane(nx, core, x, partner, out_ref, *sems)


def plane_sems(nx):
    return [pltpu.SemaphoreType.DMA((max(nx - 1, 1),))] * 2 + [pltpu.SemaphoreType.DMA((nx,))] * 2


def plane_gather(own, n, collective_id):
    nx = n // 2
    rows, wide = own.shape
    return pl.pallas_call(
        functools.partial(plane_gather_kernel, nx),
        out_shape=jax.ShapeDtypeStruct((nx, 2, rows, wide), own.dtype),
        in_specs=[pl.BlockSpec(memory_space=pltpu.VMEM)],
        out_specs=pl.BlockSpec(memory_space=pltpu.VMEM),
        scratch_shapes=plane_sems(nx),
        compiler_params=pltpu.CompilerParams(
            collective_id=collective_id, has_side_effects=True, vmem_limit_bytes=32 * 2**20
        ),
    )(own).reshape(n * rows, wide)


def plane_sum_kernel(
    nx, parts_ref, weight_ref, out_ref, half, landed, s_half, r_half, s_land, r_land, *sems
):
    core, x, partner = greet_plane(nx, lax.axis_index("col"))
    copies = []
    order = [lax.rem(x + step, nx) for step in list(range(1, nx)) + [0]]
    for step, k in enumerate(order):
        copies.append(
            send(
                parts_ref.at[k, 1 - core],
                half.at[k],
                s_half.at[step],
                r_half.at[step],
                {"col": partner},
            )
        )
        copies[-1].start()
    for step, k in enumerate(order):
        copies[step].wait_recv()
        half[k] = half[k] + parts_ref[k, core]
        if step < nx - 1:
            copies.append(
                send(
                    half.at[k],
                    landed.at[step],
                    s_land.at[step],
                    r_land.at[step],
                    {"col": k * 2 + core},
                )
            )
            copies[-1].start()
    total = half[x]
    for step in range(nx - 1):
        copies[nx + step].wait_recv()
        total = total + landed[step]
    out_ref[x, core] = total * weight_ref[...]
    spread_plane(nx, core, x, partner, out_ref, *sems)
    for copy in copies:
        copy.wait_send()


def plane_sum(partial, weight, n, collective_id):
    nx = n // 2
    rows, wide = partial.shape[0] // n, partial.shape[1]
    return pl.pallas_call(
        functools.partial(plane_sum_kernel, nx),
        out_shape=jax.ShapeDtypeStruct((nx, 2, rows, wide), partial.dtype),
        in_specs=[pl.BlockSpec(memory_space=pltpu.VMEM)] * 2,
        out_specs=pl.BlockSpec(memory_space=pltpu.VMEM),
        scratch_shapes=[
            pltpu.VMEM((nx, rows, wide), partial.dtype),
            pltpu.VMEM((max(nx - 1, 1), rows, wide), partial.dtype),
        ]
        + [pltpu.SemaphoreType.DMA((nx,))] * 2
        + [pltpu.SemaphoreType.DMA((max(nx - 1, 1),))] * 2
        + plane_sems(nx),
        compiler_params=pltpu.CompilerParams(
            collective_id=collective_id, has_side_effects=True, vmem_limit_bytes=32 * 2**20
        ),
    )(partial.reshape(nx, 2, rows, wide), weight).reshape(n * rows, wide)


def local(series, vectors, damp_class, damp_levels, removed_blocks):
    n_row, n_col = lax.axis_size("row"), lax.axis_size("col")
    row_id = lax.axis_index("row")
    col_id = lax.axis_index("col")
    shard_rows, samples = series.shape
    wide = vectors.shape[1]
    classes = damp_levels.shape[0]
    order = shard_rows * n_row * n_col
    z_own = standardize(series)
    onehot = (damp_class[:, None] == jnp.arange(classes, dtype=jnp.int32)[None, :]).astype(
        jnp.float32
    )
    damping = jnp.sum(onehot * damp_levels[None, :], axis=1)
    weight_own = damping * damping
    z_cols, z_rows = cross_gather(z_own, n_row, n_col, 0)
    z_cols, vectors = lax.optimization_barrier((z_cols, vectors))
    tile_rows, tile_cols = z_rows.shape[0], z_cols.shape[0]
    blocks = removed_blocks.shape[0]
    block_size = order // blocks
    row_blocks = tile_rows // block_size
    position = jnp.arange(tile_cols, dtype=jnp.int32)
    col_index = (position // shard_rows * n_col + col_id) * shard_rows + position % shard_rows
    col_block = col_index // block_size
    keep_rows = 1.0 - lax.dynamic_slice_in_dim(
        removed_blocks, row_id * row_blocks, row_blocks, 0
    ).astype(jnp.float32)
    col_hot = (col_block[None, :] == jnp.arange(blocks, dtype=jnp.int32)[:, None]).astype(
        jnp.float32
    )
    keep_small = jnp.dot(
        keep_rows, col_hot, precision=lax.Precision.HIGHEST, preferred_element_type=jnp.float32
    )
    keep_full = jnp.broadcast_to(
        keep_small[:, None, :], (row_blocks, block_size, tile_cols)
    ).reshape(tile_rows, tile_cols)
    rows_high, rows_low = split(z_rows)
    cols_high, cols_low = split(z_cols * (sharpness / samples))
    scores = lax.dot_general(
        jnp.concatenate([rows_high, rows_low, rows_high], axis=1),
        jnp.concatenate([cols_high, cols_high, cols_low], axis=1),
        (((1,), (1,)), ((), ())),
        preferred_element_type=jnp.float32,
    )
    t_high, t_low = split(jnp.tanh(scores) * keep_full)
    spectral_scale = 0.5 * order * jnp.mean(damp_levels * damp_levels)

    def multiply(dims, field, fine):
        high, low = split(field)
        dims = ((dims, (0,)), ((), ()))
        both = lax.dot_general(
            t_high,
            jnp.concatenate([high, low], axis=1),
            dims,
            preferred_element_type=jnp.float32,
        )
        if fine:
            both = both + lax.dot_general(
                t_low,
                jnp.concatenate([high, low], axis=1),
                dims,
                preferred_element_type=jnp.float32,
            )
        out = both[:, :wide] + both[:, wide:]
        return out

    weight_wide = jnp.broadcast_to(weight_own[:, None], (shard_rows, wide))

    def normal_apply(field_cols, fine):
        product = multiply((1,), field_cols, fine[0])
        product = plane_sum(product, weight_wide, n_col, 2)
        returned = multiply((0,), product, fine[1])
        return line_scatter(returned, n_row, 3) / spectral_scale

    vectors_cols = lax.all_gather(vectors, "row", axis=0, tiled=True)
    vectors_cols, t_high, t_low = lax.optimization_barrier((vectors_cols, t_high, t_low))
    first_term = normal_apply(vectors_cols, (True, False)) - vectors
    first_cols = line_gather(first_term, n_row, 1)
    return 2.0 * (normal_apply(first_cols, (False, True)) - first_term) - vectors


def solution(mesh):
    placed = (
        P(("ens", "row", "col"), None),
        P(("ens", "row", "col"), None),
        P(("ens", "row", "col")),
        P(),
        P("ens", None),
    )
    return jax.shard_map(
        local, mesh=mesh, in_specs=placed, out_specs=P(("ens", "row", "col"), None), check_vma=False
    )
```
